256 devices in a mesh: depth: 32 (over y_hi, z, core), res: 8 (over y_lo, x).
Axes of the slice: x: 4, y: 4 (y_hi: 2, y_lo: 2; y = y_hi * 2 + y_lo), z: 8, core: 2. Of those that a mesh axis runs over, the one named last changes fastest.
Arguments:
- alignment: bfloat16 [256, 512, 768], P('depth', 'res')
- seq_mask: int32 [256], P('depth'), may hold values from 0 to 1, as said below
- res_mask: int32 [512], P('res'), may hold values from 0 to 1, as said below
- row_query: bfloat16 [768, 768], replicated
- row_key: bfloat16 [768, 768], replicated, may hold values from -0.21875 to 0.21875
- row_value: bfloat16 [768, 768], replicated, may hold values from -0.21875 to 0.21875
- row_out: bfloat16 [768, 768], replicated, may hold values from -0.21875 to 0.21875
- col_query: bfloat16 [768, 768], replicated
- col_key: bfloat16 [768, 768], replicated, may hold values from -0.21875 to 0.21875
- col_value: bfloat16 [768, 768], replicated, may hold values from -0.21875 to 0.21875
- col_out: bfloat16 [768, 768], replicated, may hold values from -0.21875 to 0.21875
Outputs:
- layer_out: bfloat16 [256, 512, 768], P('depth', 'res')
The draws below stay inside these ranges and needn't reach their ends.
Inputs may be any that keep to these rules, and one draw needn't show every extreme that they name: `seq_mask`: 0 marks a padded sequence; sequence 0 is never padded. `res_mask`: 0 marks a padded position; position 0 is never padded.
All inputs are finite; a program needn't handle non-finite values.
Results may differ from the reference program's by a relative error of at most 0.013.
Values may be sent and summed in bfloat16 or wider, within the bound.
A program may use at most 128 MiB of HBM per device.

```python
import math
import jax
import jax.numpy as jnp
from jax import lax

D = 768
HEADS = 12
HEAD_DIM = 64
SEQS = 256
RESIDUES = 512


def draw_alignment(key, part):
    key = jax.random.fold_in(key, 1)
    return jax.random.normal(key, (SEQS, RESIDUES, D), jnp.float32).astype(jnp.bfloat16)


def scaled_matrix(key):
    return (jax.random.normal(key, (D, D), jnp.float32) * D ** (-0.5)).astype(jnp.bfloat16)


def draw_row_query(key, part):
    key = jax.random.fold_in(key, 2)
    return scaled_matrix(key)


def draw_col_query(key, part):
    key = jax.random.fold_in(key, 3)
    return scaled_matrix(key)


def padding_mask(key, length):
    picks = jax.random.randint(key, (length,), 0, 8, jnp.int32)
    marks = jnp.where(picks > 0, 1, 0).astype(jnp.int32)
    return marks.at[0].set(1)


def draw_seq_mask(key, part):
    key = jax.random.fold_in(key, 4)
    return padding_mask(key, SEQS)


def draw_res_mask(key, part):
    key = jax.random.fold_in(key, 5)
    return padding_mask(key, RESIDUES)


def noise(stream_key, extent, width, reach, kind=jnp.bfloat16):
    entries = width * jax.random.normal(stream_key, extent, jnp.float32)
    return jnp.clip(entries, min=-reach, max=reach).astype(kind)


def setup_inputs(seed: int = 0) -> dict:
    arg_keys = jax.random.split(jax.random.key(seed), 12)
    alignment = draw_alignment(jax.random.fold_in(arg_keys[11], 71), 0)
    seq_mask = draw_seq_mask(jax.random.fold_in(arg_keys[11], 71), 0)
    res_mask = draw_res_mask(jax.random.fold_in(arg_keys[11], 71), 0)
    row_query = draw_row_query(jax.random.fold_in(arg_keys[11], 71), 0)
    row_key = noise(arg_keys[4], (D, D), D ** -0.5, 0.21875)
    row_value = noise(arg_keys[5], (D, D), D ** -0.5, 0.21875)
    row_out = noise(arg_keys[6], (D, D), D ** -0.5, 0.21875)
    col_query = draw_col_query(jax.random.fold_in(arg_keys[11], 71), 0)
    col_key = noise(arg_keys[8], (D, D), D ** -0.5, 0.21875)
    col_value = noise(arg_keys[9], (D, D), D ** -0.5, 0.21875)
    col_out = noise(arg_keys[10], (D, D), D ** -0.5, 0.21875)
    return dict(alignment=alignment, seq_mask=seq_mask, res_mask=res_mask, row_query=row_query, row_key=row_key, row_value=row_value, row_out=row_out, col_query=col_query, col_key=col_key, col_value=col_value, col_out=col_out)


def layer_norm(values):
    wide = values.astype(jnp.float32)
    center = lax.optimization_barrier(jnp.mean(wide, axis=-1, keepdims=True))
    spread = lax.optimization_barrier(jnp.mean(jnp.square(wide - center), axis=-1, keepdims=True))
    return ((wide - center) * lax.rsqrt(spread + 1e-05)).astype(jnp.bfloat16)

def masked_softmax(scores, live_mask):
    alive = live_mask > 0
    largest = lax.optimization_barrier(jnp.max(jnp.where(alive, scores, -jnp.inf), axis=-1, keepdims=True))
    raised = jnp.where(alive, jnp.exp(scores - largest), 0.0)
    return (raised / lax.optimization_barrier(jnp.sum(raised, axis=-1, keepdims=True))).astype(jnp.bfloat16)

def reference(alignment, seq_mask, res_mask, row_query, row_key, row_value, row_out, col_query, col_key, col_value, col_out):
    normed = layer_norm(alignment)
    seq_live = seq_mask.astype(jnp.float32)
    row_scale = HEAD_DIM ** (-0.5) / math.sqrt(SEQS)
    queries = (jnp.dot(normed, row_query, preferred_element_type=jnp.float32) * row_scale * seq_live[:, None, None]).astype(jnp.bfloat16)
    keys = jnp.dot(normed, row_key, preferred_element_type=jnp.float32).astype(jnp.bfloat16)
    values = jnp.dot(normed, row_value, preferred_element_type=jnp.float32).astype(jnp.bfloat16)
    shape4 = (SEQS, RESIDUES, HEADS, HEAD_DIM)
    tied = jnp.einsum('rihe,rjhe->hij', queries.reshape(shape4).astype(jnp.float32), keys.reshape(shape4).astype(jnp.float32))
    row_weights = masked_softmax(tied, res_mask)
    row_mixed = jnp.einsum('hij,rjhe->rihe', row_weights.astype(jnp.float32), values.reshape(shape4).astype(jnp.float32)).astype(jnp.bfloat16)
    after_rows = (alignment.astype(jnp.float32) + jnp.dot(row_mixed.reshape(SEQS, RESIDUES, D), row_out, preferred_element_type=jnp.float32)).astype(jnp.bfloat16)
    normed_cols = layer_norm(after_rows)
    col_queries = (jnp.dot(normed_cols, col_query, preferred_element_type=jnp.float32) * HEAD_DIM ** (-0.5)).astype(jnp.bfloat16).reshape(shape4)
    col_keys = jnp.dot(normed_cols, col_key, preferred_element_type=jnp.float32).astype(jnp.bfloat16).reshape(shape4)
    col_values = jnp.dot(normed_cols, col_value, preferred_element_type=jnp.float32).astype(jnp.bfloat16).reshape(shape4)
    column_block = math.gcd(RESIDUES, 16)
    block_count = RESIDUES // column_block

    def per_block(index):
        start = (index * column_block).astype(jnp.int32)
        block_q = lax.dynamic_slice_in_dim(col_queries, start, column_block, 1).astype(jnp.float32)
        block_k = lax.dynamic_slice_in_dim(col_keys, start, column_block, 1).astype(jnp.float32)
        block_v = lax.dynamic_slice_in_dim(col_values, start, column_block, 1).astype(jnp.float32)
        scores = jnp.einsum('rche,sche->chrs', block_q, block_k)
        weights_col = masked_softmax(scores, seq_mask)
        return jnp.einsum('chrs,sche->rche', weights_col.astype(jnp.float32), block_v).astype(jnp.bfloat16)
    stacked = lax.map(per_block, jnp.arange(block_count, dtype=jnp.int32))
    col_mixed = jnp.transpose(stacked, (1, 0, 2, 3, 4)).reshape(SEQS, RESIDUES, D)
    return (after_rows.astype(jnp.float32) + jnp.dot(col_mixed, col_out, preferred_element_type=jnp.float32)).astype(jnp.bfloat16)
```

```python
import functools
import math

import jax
import jax.numpy as jnp
from jax import lax
from jax.experimental import pallas as pl
from jax.experimental.pallas import tpu as pltpu
from jax.sharding import PartitionSpec as P

HEAD = 64
LANES = 128
F32 = jnp.float32
BF16 = jnp.bfloat16
MESH = pl.DeviceIdType.MESH


class Shape:
    def __init__(self, y_hi=2, z=8, core=2, y_lo=2, x=4, seqs=8, spots=64, width=768):
        self.y_hi, self.z, self.core, self.y_lo, self.x = y_hi, z, core, y_lo, x
        self.seqs, self.spots, self.width = seqs, spots, width
        self.depth = y_hi * z * core
        self.res = y_lo * x
        self.y = y_hi * y_lo
        self.heads = width // HEAD
        self.group = self.heads // x
        self.part = seqs // y_lo
        self.wide = self.part * HEAD
        self.all_spots = self.res * spots
        self.tied_rows = self.group * self.all_spots
        self.half = self.all_spots // core
        self.block = self.tied_rows // (self.z * self.y)
        self.rows = seqs * spots
        self.per = spots // self.depth
        self.msg = self.per * seqs
        self.up = self.z // 2
        self.down = (self.z - 1) // 2


def remote(src, dst, send, recv, device):
    return pltpu.make_async_remote_copy(
        src_ref=src, dst_ref=dst, send_sem=send, recv_sem=recv, device_id=device, device_id_type=MESH
    )


def normalise(wide):
    center = jnp.mean(wide, axis=-1, keepdims=True)
    moved = wide - center
    spread = jnp.mean(jnp.square(moved), axis=-1, keepdims=True)
    return moved * lax.rsqrt(spread + 1e-05)


def nt_dot(a, b):
    return lax.dot_general(a, b, (((1,), (1,)), ((), ())), preferred_element_type=F32)


def dot(a, b):
    return jnp.dot(a, b, preferred_element_type=F32)


def low_half(shape):
    return lax.broadcasted_iota(jnp.int32, shape, len(shape) - 1) % LANES < HEAD


def swap_halves(first, second):
    low = low_half(first.shape)
    return (
        jnp.where(low, first, pltpu.roll(second, HEAD, 1)),
        jnp.where(low, pltpu.roll(first, HEAD, 1), second),
    )


def chunk_of(total, limit):
    size = min(total, limit)
    while total % size:
        size //= 2
    return size


def row_kernel(
    sh,
    x_ref,
    marks_ref,
    wq_ref,
    wk_ref,
    wv_ref,
    wo_ref,
    after_ref,
    perm_ref,
    seqs_ref,
    normed,
    send_k,
    send_q,
    send_v,
    got_k,
    got_q,
    got_v,
    res_marks,
    tied,
    pair,
    up_buf,
    down_buf,
    y1_src,
    y1_buf,
    y2_buf,
    z2_src,
    z2_buf,
    own,
    other,
    weights,
    mixed,
    back,
    gathered,
    mark_send,
    mark_recv,
    res_send,
    res_recv,
    qkv_send,
    qkv_recv,
    local_sem,
    pair_send,
    pair_recv,
    up_send,
    up_recv,
    down_send,
    down_recv,
    y_send,
    y_recv,
    z_send,
    z_recv,
    gup_send,
    gup_recv,
    gdown_send,
    gdown_recv,
    back_send,
    back_recv,
):
    d = lax.axis_index("depth")
    m = lax.axis_index("res")
    core = d % sh.core
    z = (d // sh.core) % sh.z
    y_hi = d // (sh.core * sh.z)
    x = m % sh.x
    y_lo = m // sh.x
    y = y_hi * sh.y_lo + y_lo
    mate = 1 - core

    def at_depth(k):
        return (
            ((y_hi + k // (sh.z * sh.core)) % sh.y_hi) * (sh.z * sh.core)
            + ((z + (k // sh.core) % sh.z) % sh.z) * sh.core
            + (core + k % sh.core) % sh.core
        )

    def at_res(k):
        return ((y_lo + k // sh.x) % sh.y_lo) * sh.x + (x + k % sh.x) % sh.x

    def at_z(k):
        return (y_hi * sh.z + (z + k + sh.z) % sh.z) * sh.core + core

    def at_y(k):
        there = (y + k) % sh.y
        return ((there // sh.y_lo) * sh.z + z) * sh.core + core, (there % sh.y_lo) * sh.x + x, there

    mate_id = ((y_hi * sh.z + z) * sh.core + mate, m)

    barrier = pltpu.get_barrier_semaphore()

    def greet_depth(k, c):
        pl.semaphore_signal(barrier, inc=1, device_id=(at_depth(k), m), device_id_type=MESH)
        return c

    lax.fori_loop(1, sh.depth, greet_depth, 0)

    def greet_res(k, c):
        pl.semaphore_signal(barrier, inc=1, device_id=(d, at_res(k)), device_id_type=MESH)
        return c

    lax.fori_loop(1, sh.res, greet_res, 0)
    for k in range(1, sh.y):
        dy, ry, _ = at_y(k)
        pl.semaphore_signal(barrier, inc=1, device_id=(dy, ry), device_id_type=MESH)
    pl.semaphore_wait(barrier, sh.depth - 1 + sh.res - 1 + sh.y - 1)

    seqs_ref[pl.ds(d, 1)] = marks_ref[1:2]
    res_marks[pl.ds(m, 1)] = marks_ref[0:1]

    def mark_copy(k):
        return remote(
            marks_ref.at[1], seqs_ref.at[d], mark_send.at[k], mark_recv.at[k], (at_depth(k), m)
        )

    def res_copy(k):
        return remote(
            marks_ref.at[0], res_marks.at[m], res_send.at[k], res_recv.at[k], (d, at_res(k))
        )

    lax.fori_loop(1, sh.depth, lambda k, c: (mark_copy(k).start(), c)[1], 0)
    lax.fori_loop(1, sh.res, lambda k, c: (res_copy(k).start(), c)[1], 0)

    step = sh.spots

    def norm_rows(r, c):
        rows = pl.ds(pl.multiple_of(r * step, step), step)
        normed[rows, :] = normalise(x_ref[rows, :].astype(F32)).astype(BF16)
        return c

    lax.fori_loop(0, sh.seqs, norm_rows, 0)

    part_rows = sh.part * sh.spots
    ncol = chunk_of(sh.width, 256)

    def project(w_ref, out_ref, scale):
        def half(s, c):
            rows = pl.ds(pl.multiple_of(s * part_rows, part_rows), part_rows)
            for n in range(sh.width // ncol):
                res = dot(normed[rows, :], w_ref[:, n * ncol : (n + 1) * ncol])
                tiles = []
                for r in range(sh.part):
                    t = res[r * sh.spots : (r + 1) * sh.spots]
                    if scale is not None:
                        live = marks_ref[1, pl.ds(s * sh.part + r, 1), :]
                        t = t * (jnp.tile(live, (1, ncol // LANES)) * scale)
                    tiles.append(t)
                for p in range(ncol // LANES):
                    lanes = slice(p * LANES, (p + 1) * LANES)
                    head = (n * ncol + p * LANES) // HEAD
                    for rp in range(sh.part // 2):
                        even, odd = swap_halves(tiles[2 * rp][:, lanes], tiles[2 * rp + 1][:, lanes])
                        to = slice(rp * LANES, (rp + 1) * LANES)
                        for h, t in ((head, even), (head + 1, odd)):
                            out_ref[s * sh.x + h // sh.group, h % sh.group, :, to] = t.astype(BF16)
            return c

        lax.fori_loop(0, sh.y_lo, half, 0)

    def qkv_copy(i, src, dst, k):
        there = at_res(k)
        return remote(
            src.at[there], dst.at[:, m], qkv_send.at[i, k], qkv_recv.at[i, k], (d, there)
        )

    def own_copy(i, src, dst):
        return pltpu.make_async_copy(src.at[m], dst.at[:, m], local_sem.at[i])

    sets = ((0, send_k, got_k, wk_ref, None), (1, send_q, got_q, wq_ref, None), (2, send_v, got_v, wv_ref, None))
    row_scale = HEAD ** (-0.5) / math.sqrt(sh.depth * sh.seqs)
    for i, src, dst, w_ref, _ in sets:
        project(w_ref, src, row_scale if i == 1 else None)
        own_copy(i, src, dst).start()
        lax.fori_loop(1, sh.res, lambda k, c: (qkv_copy(i, src, dst, k).start(), c)[1], 0)

    def arrive_qkv(i, src, dst):
        own_copy(i, src, dst).wait()

        def one(k, c):
            back_m = ((y_lo + sh.y_lo - k // sh.x) % sh.y_lo) * sh.x + (x + sh.x - k % sh.x) % sh.x
            remote(
                src.at[0], dst.at[:, back_m], qkv_send.at[i, k], qkv_recv.at[i, k], (d, back_m)
            ).wait_recv()
            return c

        lax.fori_loop(1, sh.res, one, 0)

    arrive_qkv(0, send_k, got_k)
    arrive_qkv(1, send_q, got_q)

    for h in range(sh.group):
        q = got_q[h].reshape(sh.all_spots, sh.wide)
        for j in range(sh.core):
            per_half = sh.res // sh.core
            k = got_k[h, j * per_half : (j + 1) * per_half].reshape(sh.half, sh.wide)
            res = nt_dot(q, k)
            zs = sh.z * sh.y // sh.group
            tied[j, h * sh.all_spots : (h + 1) * sh.all_spots, :] = res

    half_copy = remote(tied.at[mate], pair, pair_send.at[0], pair_recv.at[0], mate_id)
    half_copy.start()
    half_copy.wait_recv()
    rows_z = sh.y * sh.block
    tied_step = sh.block

    def add_pair(t, c):
        rows = pl.ds(pl.multiple_of(t * tied_step, tied_step), tied_step)
        pair[rows, :] = pair[rows, :] + tied[core, rows, :]
        return c

    lax.fori_loop(0, sh.tied_rows // tied_step, add_pair, 0)

    low = pl.ds(0, LANES)
    high = pl.ds(LANES, LANES)

    def z_rows(k):
        return pl.ds(pl.multiple_of(((z + k + sh.z) % sh.z) * rows_z, rows_z), rows_z)

    def block_rows(zz, yy):
        return pl.ds(pl.multiple_of(zz * rows_z + yy * sh.block, sh.block), sh.block)

    def y2_copies(k):
        dy, ry, there = at_y(k)
        return [
            remote(
                pair.at[block_rows(zz, there), high],
                y2_buf.at[k - 1, zz],
                y_send.at[0, k, zz],
                y_recv.at[0, k, zz],
                (dy, ry),
            )
            for zz in range(sh.z)
        ]

    def up_copy(t):
        src = pair.at[z_rows(sh.up), low] if t == 0 else up_buf.at[t - 1]
        return remote(src, up_buf.at[t], up_send.at[t], up_recv.at[t], (at_z(1), m))

    def down_copy(t):
        src = pair.at[z_rows(-sh.down), low] if t == 0 else down_buf.at[t - 1]
        return remote(src, down_buf.at[t], down_send.at[t], down_recv.at[t], (at_z(-1), m))

    def z2_copy(k):
        there = (z + k) % sh.z
        return remote(
            z2_src.at[there], z2_buf.at[k - 1], z_send.at[0, k], z_recv.at[0, k], (at_z(k), m)
        )

    def y1_copy(k):
        dy, ry, there = at_y(k)
        return remote(
            y1_src.at[there], y1_buf.at[k - 1], y_send.at[1, k, 0], y_recv.at[1, k, 0], (dy, ry)
        )

    up_copy(0).start()
    if sh.down:
        down_copy(0).start()
    for k in range(1, sh.y):
        for c in y2_copies(k):
            c.start()
    for t in range(1, sh.up):
        up_copy(t - 1).wait_recv()
        up_buf[t - 1] = up_buf[t - 1] + pair[z_rows(sh.up - t), low]
        up_copy(t).start()
        if t < sh.down:
            down_copy(t - 1).wait_recv()
            down_buf[t - 1] = down_buf[t - 1] + pair[z_rows(t - sh.down), low]
            down_copy(t).start()
    for k in range(1, sh.y):
        for c in y2_copies(k):
            c.wait_recv()
    for zz in range(sh.z):
        total = pair[block_rows(zz, y), high]
        for k in range(1, sh.y):
            total = total + y2_buf[k - 1, zz]
        z2_src[zz] = total
    for k in range(1, sh.z):
        z2_copy(k).start()
    up_copy(sh.up - 1).wait_recv()
    if sh.down:
        down_copy(sh.down - 1).wait_recv()
    total = pair[z_rows(0), low] + up_buf[sh.up - 1]
    if sh.down:
        total = total + down_buf[sh.down - 1]
    y1_src[...] = total.reshape(sh.y, sh.block, LANES)
    for k in range(1, sh.y):
        y1_copy(k).start()
    for k in range(1, sh.y):
        y1_copy(k).wait_recv()
    total = y1_src[y]
    for k in range(1, sh.y):
        total = total + y1_buf[k - 1]
    own[:, 0:LANES] = total
    for k in range(1, sh.z):
        z2_copy(k).wait_recv()
    total = z2_src[z]
    for k in range(1, sh.z):
        total = total + z2_buf[k - 1]
    own[:, LANES : 2 * LANES] = total

    own_pair = remote(own, other, pair_send.at[1], pair_recv.at[1], mate_id)
    own_pair.start()

    def res_arrive(k, c):
        back_m = ((y_lo + sh.y_lo - k // sh.x) % sh.y_lo) * sh.x + (x + sh.x - k % sh.x) % sh.x
        remote(
            marks_ref.at[0], res_marks.at[back_m], res_send.at[k], res_recv.at[k], (d, back_m)
        ).wait_recv()
        return c

    lax.fori_loop(1, sh.res, res_arrive, 0)

    def live_columns(which):
        per_half = sh.res // sh.core
        tiles = []
        for p in range(per_half // 2):
            first = res_marks[which * per_half + 2 * p]
            second = res_marks[which * per_half + 2 * p + 1]
            tiles.append(jnp.where(low_half(first.shape), first, second))
        return jnp.concatenate(tiles, axis=1)[0:1]

    own_live = live_columns(core) > 0.0
    other_live = live_columns(mate) > 0.0
    own_pair.wait_recv()
    own_s = jnp.where(own_live, own[...], -jnp.inf)
    other_s = jnp.where(other_live, other[...], -jnp.inf)
    top = jnp.maximum(
        jnp.max(own_s, axis=-1, keepdims=True), jnp.max(other_s, axis=-1, keepdims=True)
    )
    own_e = jnp.exp(own_s - top)
    other_e = jnp.exp(other_s - top)
    sums = jnp.sum(own_e, axis=-1, keepdims=True) + jnp.sum(other_e, axis=-1, keepdims=True)
    weights[core, block_rows(z, y), :] = (own_e / sums).astype(BF16)

    def gz_copy(k, zz):
        rows = block_rows(zz, y)
        ref = weights.at[core, rows, low]
        return remote(ref, ref, z_send.at[1, k], z_recv.at[1, k], (at_z(k), m))

    def gy_copy(k, yy):
        dy, ry, _ = at_y(k)
        rows = block_rows(z, yy)
        ref = weights.at[core, rows, high]
        return remote(ref, ref, y_send.at[2, k, 0], y_recv.at[2, k, 0], (dy, ry))

    def gy_all(k, yy):
        dy, ry, _ = at_y(k)
        copies = []
        for zz in range(sh.z):
            ref = weights.at[core, block_rows(zz, yy), low]
            copies.append(remote(ref, ref, y_send.at[3, k, zz], y_recv.at[3, k, zz], (dy, ry)))
        return copies

    def gup_copy(t, came):
        ref = weights.at[core, z_rows(-t - came), high]
        return remote(ref, ref, gup_send.at[t], gup_recv.at[t], (at_z(1), m))

    def gdown_copy(t, came):
        ref = weights.at[core, z_rows(t + came), high]
        return remote(ref, ref, gdown_send.at[t], gdown_recv.at[t], (at_z(-1), m))

    for k in range(1, sh.y):
        gy_copy(k, y).start()
    for k in range(1, sh.z):
        gz_copy(k, z).start()
    for k in range(1, sh.y):
        gy_copy(k, (y + sh.y - k) % sh.y).wait_recv()
    gup_copy(0, 0).start()
    if sh.down:
        gdown_copy(0, 0).start()
    for k in range(1, sh.z):
        gz_copy(k, (z + sh.z - k) % sh.z).wait_recv()
    for k in range(1, sh.y):
        for c in gy_all(k, y):
            c.start()
    for t in range(1, sh.up):
        gup_copy(t - 1, 1).wait_recv()
        gup_copy(t, 0).start()
        if t < sh.down:
            gdown_copy(t - 1, 1).wait_recv()
            gdown_copy(t, 0).start()
    gup_copy(sh.up - 1, 1).wait_recv()
    if sh.down:
        gdown_copy(sh.down - 1, 1).wait_recv()
    for k in range(1, sh.y):
        for c in gy_all(k, (y + sh.y - k) % sh.y):
            c.wait_recv()
    weights_pair = remote(
        weights.at[core], weights.at[core], pair_send.at[2], pair_recv.at[2], mate_id
    )
    weights_pair.start()
    arrive_qkv(2, send_v, got_v)
    remote(
        weights.at[mate], weights.at[mate], pair_send.at[2], pair_recv.at[2], mate_id
    ).wait_recv()

    for h in range(sh.group):
        v = got_v[h].reshape(sh.all_spots, sh.wide)
        rows = slice(h * sh.all_spots, (h + 1) * sh.all_spots)
        total = dot(weights[0, rows, :], v[: sh.half])
        for j in range(1, sh.core):
            total = total + dot(weights[j, rows, :], v[j * sh.half : (j + 1) * sh.half])
        mixed[h] = total.astype(BF16).reshape(sh.res, sh.spots, sh.wide)

    def back_copy(k, there, here):
        return remote(
            mixed.at[:, there], back.at[here], back_send.at[k], back_recv.at[k], (d, there)
        )

    home = pltpu.make_async_copy(mixed.at[:, m], back.at[m], local_sem.at[3])
    home.start()
    lax.fori_loop(1, sh.res, lambda k, c: (back_copy(k, at_res(k), m).start(), c)[1], 0)
    home.wait()

    def back_arrive(k, c):
        back_m = ((y_lo + sh.y_lo - k // sh.x) % sh.y_lo) * sh.x + (x + sh.x - k % sh.x) % sh.x
        back_copy(k, back_m, back_m).wait_recv()
        return c

    lax.fori_loop(1, sh.res, back_arrive, 0)

    def unpack(s, c):
        for p in range(sh.heads // 2):
            for rp in range(sh.part // 2):
                lanes = slice(rp * LANES, (rp + 1) * LANES)
                tiles = []
                for h in (2 * p, 2 * p + 1):
                    tiles.append(
                        back[s * sh.x + h // sh.group, h % sh.group, :, lanes].astype(F32)
                    )
                first, second = swap_halves(*tiles)
                for r, t in ((0, first), (1, second)):
                    row = (s * sh.part + 2 * rp + r) * sh.spots
                    gathered[
                        pl.ds(pl.multiple_of(row, sh.spots), sh.spots), p * LANES : (p + 1) * LANES
                    ] = t.astype(BF16)
        return c

    lax.fori_loop(0, sh.y_lo, unpack, 0)

    def close_rows(s, c):
        rows = pl.ds(pl.multiple_of(s * part_rows, part_rows), part_rows)
        after = (x_ref[rows, :].astype(F32) + dot(gathered[rows, :], wo_ref[...])).astype(BF16)
        after_ref[rows, :] = after
        normed[rows, :] = normalise(after.astype(F32)).astype(BF16)
        return c

    lax.fori_loop(0, sh.y_lo, close_rows, 0)

    prow = chunk_of(sh.rows, 256)

    def permute(t, c):
        a = lax.broadcasted_iota(jnp.int32, (prow, sh.rows), 0) + t * prow
        b = lax.broadcasted_iota(jnp.int32, (prow, sh.rows), 1)
        pick = jnp.where(b == (a % sh.seqs) * sh.spots + a // sh.seqs, 1.0, 0.0).astype(BF16)
        perm_ref[pl.ds(pl.multiple_of(t * prow, prow), prow), :] = dot(pick, normed[...]).astype(BF16)
        return c

    lax.fori_loop(0, sh.rows // prow, permute, 0)

    def seqs_arrive(k, c):
        back_d = (
            ((y_hi + sh.y_hi - k // (sh.z * sh.core)) % sh.y_hi) * (sh.z * sh.core)
            + ((z + sh.z - (k // sh.core) % sh.z) % sh.z) * sh.core
            + (core + sh.core - k % sh.core) % sh.core
        )
        remote(
            marks_ref.at[1], seqs_ref.at[back_d], mark_send.at[k], mark_recv.at[k], (back_d, m)
        ).wait_recv()
        mark_copy(k).wait_send()
        return c

    lax.fori_loop(1, sh.depth, seqs_arrive, 0)

    def sent_res(k, c):
        res_copy(k).wait_send()
        for i, src, dst, _, _ in sets:
            qkv_copy(i, src, dst, k).wait_send()
        back_copy(k, at_res(k), m).wait_send()
        return c

    lax.fori_loop(1, sh.res, sent_res, 0)
    half_copy.wait_send()
    own_pair.wait_send()
    weights_pair.wait_send()
    for t in range(sh.up):
        up_copy(t).wait_send()
        gup_copy(t, 0).wait_send()
    for t in range(sh.down):
        down_copy(t).wait_send()
        gdown_copy(t, 0).wait_send()
    for k in range(1, sh.y):
        for c in y2_copies(k):
            c.wait_send()
        for c in gy_all(k, y):
            c.wait_send()
        y1_copy(k).wait_send()
        gy_copy(k, y).wait_send()
    for k in range(1, sh.z):
        z2_copy(k).wait_send()
        gz_copy(k, z).wait_send()


def column_kernel(
    sh,
    perm_ref,
    after_ref,
    seqs_ref,
    wq_ref,
    wk_ref,
    wv_ref,
    wo_ref,
    out_ref,
    rows_in,
    q_buf,
    k_buf,
    v_buf,
    wide,
    rows_out,
    rows_back,
    straight,
    in_send,
    in_recv,
    out_send,
    out_recv,
    local_sem,
):
    d = lax.axis_index("depth")
    m = lax.axis_index("res")
    core = d % sh.core
    z = (d // sh.core) % sh.z
    y_hi = d // (sh.core * sh.z)

    def at_depth(k):
        return (
            ((y_hi + k // (sh.z * sh.core)) % sh.y_hi) * (sh.z * sh.core)
            + ((z + (k // sh.core) % sh.z) % sh.z) * sh.core
            + (core + k % sh.core) % sh.core
        )

    def from_depth(k):
        return (
            ((y_hi + sh.y_hi - k // (sh.z * sh.core)) % sh.y_hi) * (sh.z * sh.core)
            + ((z + sh.z - (k // sh.core) % sh.z) % sh.z) * sh.core
            + (core + sh.core - k % sh.core) % sh.core
        )

    barrier = pltpu.get_barrier_semaphore()

    def greet(k, c):
        pl.semaphore_signal(barrier, inc=1, device_id=(at_depth(k), m), device_id_type=MESH)
        return c

    lax.fori_loop(1, sh.depth, greet, 0)
    pl.semaphore_wait(barrier, sh.depth - 1)

    def in_copy(k, there, here):
        return remote(
            perm_ref.at[there], rows_in.at[here], in_send.at[k], in_recv.at[k], (there, m)
        )

    own = pltpu.make_async_copy(perm_ref.at[d], rows_in.at[d], local_sem.at[0])
    own.start()
    lax.fori_loop(1, sh.depth, lambda k, c: (in_copy(k, at_depth(k), d).start(), c)[1], 0)
    own.wait()

    def in_arrive(k, c):
        in_copy(k, from_depth(k), from_depth(k)).wait_recv()
        return c

    lax.fori_loop(1, sh.depth, in_arrive, 0)

    seqs = sh.depth * sh.seqs
    rows = rows_in[...].reshape(sh.depth * sh.msg, sh.width)
    ncol = chunk_of(sh.width, 256)
    for w_ref, to, scale in ((wq_ref, q_buf, HEAD ** (-0.5)), (wk_ref, k_buf, None), (wv_ref, v_buf, None)):
        for n in range(sh.width // ncol):
            lanes = slice(n * ncol, (n + 1) * ncol)
            res = dot(rows, w_ref[:, lanes])
            if scale is not None:
                res = res * scale
            res = res.reshape(sh.depth, sh.per, sh.seqs, ncol)
            for p in range(sh.per):
                to[p, :, lanes] = res[:, p].reshape(seqs, ncol).astype(BF16)

    pick = jnp.where(
        lax.broadcasted_iota(jnp.int32, (8, LANES), 1) == 0, 1.0, 0.0
    ).astype(F32)
    alive = nt_dot(pick, seqs_ref[...].reshape(seqs, LANES))[0:1] > 0.5

    def attend(p, c):
        for pair in range(sh.heads // 2):
            lanes = slice(pair * LANES, (pair + 1) * LANES)
            q = q_buf[p, :, lanes]
            k = k_buf[p, :, lanes]
            v = v_buf[p, :, lanes]
            low = low_half(q.shape)
            halves = []
            for keep in (low, jnp.logical_not(low)):
                scores = nt_dot(jnp.where(keep, q, jnp.zeros_like(q)), k)
                scores = jnp.where(alive, scores, -jnp.inf)
                raised = jnp.exp(scores - jnp.max(scores, axis=-1, keepdims=True))
                share = (raised / jnp.sum(raised, axis=-1, keepdims=True)).astype(BF16)
                halves.append(dot(share, v))
            mixed = jnp.where(low, halves[0], halves[1])
            wide[:, p, :, lanes] = mixed.reshape(sh.depth, sh.seqs, LANES)
        return c

    lax.fori_loop(0, sh.per, attend, 0)
    rows_out[...] = wide[...].reshape(sh.depth, sh.msg, sh.width).astype(BF16)

    def out_copy(k, there, here):
        return remote(
            rows_out.at[there], rows_back.at[here], out_send.at[k], out_recv.at[k], (there, m)
        )

    own_back = pltpu.make_async_copy(rows_out.at[d], rows_back.at[d], local_sem.at[1])
    own_back.start()
    lax.fori_loop(1, sh.depth, lambda k, c: (out_copy(k, at_depth(k), d).start(), c)[1], 0)
    own_back.wait()

    def out_arrive(k, c):
        out_copy(k, from_depth(k), from_depth(k)).wait_recv()
        return c

    lax.fori_loop(1, sh.depth, out_arrive, 0)

    prow = chunk_of(sh.rows, 256)

    def finish(t, c):
        part = pl.ds(pl.multiple_of(t * prow, prow), prow)
        a = lax.broadcasted_iota(jnp.int32, (prow, sh.rows), 0) + t * prow
        b = lax.broadcasted_iota(jnp.int32, (prow, sh.rows), 1)
        pick = jnp.where(b == (a % sh.spots) * sh.seqs + a // sh.spots, 1.0, 0.0).astype(BF16)
        straight[part, :] = dot(pick, rows_back[...].reshape(sh.rows, sh.width)).astype(BF16)
        out_ref[part, :] = (
            after_ref[part, :].astype(F32) + dot(straight[part, :], wo_ref[...])
        ).astype(BF16)
        return c

    lax.fori_loop(0, sh.rows // prow, finish, 0)

    def sent(k, c):
        in_copy(k, at_depth(k), d).wait_send()
        out_copy(k, at_depth(k), d).wait_send()
        return c

    lax.fori_loop(1, sh.depth, sent, 0)


def body(sh, alignment, seq_mask, res_mask, rq, rk, rv, ro, cq, ck, cv, co):
    x = alignment.reshape(sh.rows, sh.width)
    spot_marks = jnp.broadcast_to(jnp.tile(res_mask, LANES // sh.spots)[None], (8, LANES))
    seq_marks = jnp.broadcast_to(seq_mask[:, None], (sh.seqs, LANES))
    marks = jnp.stack([spot_marks, seq_marks]).astype(F32)
    vmem = pl.BlockSpec(memory_space=pltpu.VMEM)
    dma = lambda *s: pltpu.SemaphoreType.DMA(s)
    packed = (sh.group, sh.res, sh.spots, sh.wide)
    to_peers = (sh.res, sh.group, sh.spots, sh.wide)
    rows_z = sh.y * sh.block
    down = max(sh.down, 1)
    after, perm, seqs = pl.pallas_call(
        functools.partial(row_kernel, sh),
        out_shape=(
            jax.ShapeDtypeStruct((sh.rows, sh.width), BF16),
            jax.ShapeDtypeStruct((sh.rows, sh.width), BF16),
            jax.ShapeDtypeStruct((sh.depth, 8, LANES), F32),
        ),
        in_specs=[vmem] * 6,
        out_specs=(vmem,) * 3,
        scratch_shapes=[
            pltpu.VMEM((sh.rows, sh.width), BF16),
            pltpu.VMEM(to_peers, BF16),
            pltpu.VMEM(to_peers, BF16),
            pltpu.VMEM(to_peers, BF16),
            pltpu.VMEM(packed, BF16),
            pltpu.VMEM(packed, BF16),
            pltpu.VMEM(packed, BF16),
            pltpu.VMEM((sh.res, 8, LANES), F32),
            pltpu.VMEM((sh.core, sh.tied_rows, sh.half), F32),
            pltpu.VMEM((sh.tied_rows, sh.half), F32),
            pltpu.VMEM((sh.up, rows_z, LANES), F32),
            pltpu.VMEM((down, rows_z, LANES), F32),
            pltpu.VMEM((sh.y, sh.block, LANES), F32),
            pltpu.VMEM((sh.y - 1, sh.block, LANES), F32),
            pltpu.VMEM((sh.y - 1, sh.z, sh.block, LANES), F32),
            pltpu.VMEM((sh.z, sh.block, LANES), F32),
            pltpu.VMEM((sh.z - 1, sh.block, LANES), F32),
            pltpu.VMEM((sh.block, sh.half), F32),
            pltpu.VMEM((sh.block, sh.half), F32),
            pltpu.VMEM((sh.core, sh.tied_rows, sh.half), BF16),
            pltpu.VMEM(packed, BF16),
            pltpu.VMEM(to_peers, BF16),
            pltpu.VMEM((sh.rows, sh.width), BF16),
            dma(sh.depth),
            dma(sh.depth),
            dma(sh.res),
            dma(sh.res),
            dma(3, sh.res),
            dma(3, sh.res),
            dma(4),
            dma(3),
            dma(3),
            dma(sh.up),
            dma(sh.up),
            dma(down),
            dma(down),
            dma(4, sh.y, sh.z),
            dma(4, sh.y, sh.z),
            dma(2, sh.z),
            dma(2, sh.z),
            dma(sh.up),
            dma(sh.up),
            dma(down),
            dma(down),
            dma(sh.res),
            dma(sh.res),
        ],
        compiler_params=pltpu.CompilerParams(
            collective_id=0, has_side_effects=True, vmem_limit_bytes=56 * 2**20
        ),
        name="rows",
    )(x, marks, rq, rk, rv, ro)

    seqs_all = sh.depth * sh.seqs
    message = (sh.depth, sh.msg, sh.width)
    by_spot = (sh.per, seqs_all, sh.width)
    out = pl.pallas_call(
        functools.partial(column_kernel, sh),
        out_shape=jax.ShapeDtypeStruct((sh.rows, sh.width), BF16),
        in_specs=[vmem] * 7,
        out_specs=vmem,
        scratch_shapes=[
            pltpu.VMEM(message, BF16),
            pltpu.VMEM(by_spot, BF16),
            pltpu.VMEM(by_spot, BF16),
            pltpu.VMEM(by_spot, BF16),
            pltpu.VMEM((sh.depth, sh.per, sh.seqs, sh.width), F32),
            pltpu.VMEM(message, BF16),
            pltpu.VMEM(message, BF16),
            pltpu.VMEM((sh.rows, sh.width), BF16),
            dma(sh.depth),
            dma(sh.depth),
            dma(sh.depth),
            dma(sh.depth),
            dma(2),
        ],
        compiler_params=pltpu.CompilerParams(
            collective_id=1, has_side_effects=True, vmem_limit_bytes=56 * 2**20
        ),
        name="columns",
    )(perm.reshape(message), after, seqs, cq, ck, cv, co)
    return out.reshape(alignment.shape)


def build(mesh, sh):
    placed = (P("depth", "res", None), P("depth"), P("res"), P(), P(), P(), P(), P(), P(), P(), P())
    return jax.shard_map(
        functools.partial(body, sh),
        mesh=mesh,
        in_specs=placed,
        out_specs=P("depth", "res", None),
        check_vma=False,
    )


def solution(mesh):
    return build(mesh, Shape())
```
